32 devices in a mesh: groups: 2 (over y), gx: 8 (over z, x), gy: 2 (over core).
Axes of the slice: x: 2, y: 2, z: 4, core: 2. Of those that a mesh axis runs over, the one named last changes fastest.
Arguments:
- tokens: bfloat16 [32, 16384], P(('groups', 'gx'), 'gy'), parts along dimension 0, may hold values from -6 to 6
- query_weight: bfloat16 [12288, 16384], P('gx', 'gy'), may hold values from -0.046875 to 0.046875
- key_weight: bfloat16 [768, 16384], P('gx', 'gy'), may hold values from -0.046875 to 0.046875
- value_weight: bfloat16 [768, 16384], P('gx', 'gy'), may hold values from -0.046875 to 0.046875
- output_weight: bfloat16 [16384, 12288], P('gx', 'gy'), may hold values from -0.0546875 to 0.0546875
- key_cache: bfloat16 [32, 6, 256, 128], P(('groups', 'gx'), 'gy'), parts along dimension 0, may hold values from -68 to 68
- value_cache: bfloat16 [32, 6, 256, 128], P(('groups', 'gx'), 'gy'), parts along dimension 0, may hold values from -6 to 6
- lengths: int32 [32], P(('groups', 'gx')), parts along dimension 0, may hold values from 1 to 256, as said below
Outputs:
- block_out: bfloat16 [32, 16384], P(('groups', 'gy'), 'gx'), parts along dimension 0
The draws below stay inside these ranges and needn't reach their ends.
There are 2 independent parts, one for each index of `groups`. The reference program is written for one: setup_inputs(seed, part) draws one part's arguments, and reference() takes and returns one part's arrays. A program takes and returns all parts, laid end to end along the dimension named above; an argument that names none is the same for every part. Nothing has to cross between parts.
Inputs may be any that keep to these rules, and one draw needn't show every extreme that they name: `lengths`: every row has at least one cached token and some row of every draw has exactly 256.
All inputs are finite; a program needn't handle non-finite values.
Results may differ from the reference program's by a relative error of at most 0.0082.
Values may be sent and summed in bfloat16 or wider, within the bound.
A program may use at most 128 MiB of HBM per device.

```python
import math
import jax
import jax.numpy as jnp
from jax import lax

D = 16384
HD = 128
HQ = 96
KVH = 6
CACHE_LEN = 256
ROWS = 16


def draw_key_cache(key, part):
    key = jax.random.fold_in(key, 3)
    key_base = jax.random.fold_in(key, 0)
    shape = (ROWS, KVH, CACHE_LEN, HD)
    values = jnp.clip(jax.random.normal(key_base, shape, jnp.float32), -6.0, 6.0)
    return values.astype(jnp.bfloat16)


def draw_lengths(key, part):
    key = jax.random.fold_in(key, 7)
    key_one, key_two, key_three, key_row = jax.random.split(key, 4)
    first = jax.random.randint(key_one, (ROWS,), 1, CACHE_LEN + 1)
    second = jax.random.randint(key_two, (ROWS,), 1, CACHE_LEN + 1)
    third = jax.random.randint(key_three, (ROWS,), 1, CACHE_LEN + 1)
    shortest = jnp.minimum(first, jnp.minimum(second, third))
    chosen = jax.random.randint(key_row, (), 0, ROWS)
    return jnp.where(jnp.arange(ROWS) == chosen, CACHE_LEN, shortest).astype(jnp.int32)


def shard_levels(key, shape, cuts, smallest, high):
    gain, own = 1.0, jax.random.fold_in(key, 6)
    for axis_at, shards_of in cuts:
        steps = jnp.exp(jax.random.uniform(jax.random.fold_in(own, axis_at), (shards_of,), jnp.float32, smallest / len(cuts), high / len(cuts)))
        gain = gain * jnp.repeat(steps, shape[axis_at] // shards_of).reshape([-1 if axis == axis_at else 1 for axis in range(len(shape))])
    return gain


def noise(own_key, dims, scale, reach, pieces=(), held_as=jnp.bfloat16):
    level = shard_levels(own_key, dims, pieces, -0.22, 0.18) if pieces else 1.0
    entries = jax.random.normal(own_key, dims, jnp.float32) * scale * level
    return jnp.minimum(jnp.maximum(entries, -reach), reach).astype(held_as)


def setup_inputs(seed: int = 0, part: int = 0) -> dict:
    key_list = jax.random.split(jax.random.key(seed), 9)
    part_keys = jax.random.split(jax.random.fold_in(key_list[8], part), 9)
    return {
        "tokens": noise(part_keys[0], (ROWS, D), 1.0, 6.0, ((0, 8), (1, 2))),
        "query_weight": noise(key_list[1], (HQ * HD, D), D ** -0.5, 0.046875, ((0, 8), (1, 2))),
        "key_weight": noise(key_list[2], (KVH * HD, D), D ** -0.5, 0.046875, ((0, 8), (1, 2))),
        "value_weight": noise(key_list[3], (KVH * HD, D), D ** -0.5, 0.046875, ((0, 8), (1, 2))),
        "output_weight": noise(key_list[4], (D, HQ * HD), (HQ * HD) ** -0.5, 0.0546875, ((0, 8), (1, 2))),
        "key_cache": draw_key_cache(jax.random.fold_in(jax.random.fold_in(key_list[8], part), 71), part),
        "value_cache": noise(part_keys[6], (ROWS, KVH, CACHE_LEN, HD), 1.0, 6.0, ((0, 8), (1, 2))),
        "lengths": draw_lengths(jax.random.fold_in(jax.random.fold_in(key_list[8], part), 71), part),
    }


def rotate(values, positions):
    half_width = values.shape[-1] // 2
    freqs = jnp.exp(-(jnp.arange(half_width, dtype=jnp.float32) * (2.0 / values.shape[-1])) * math.log(500000.0))
    angles = positions[:, None] * freqs[None, :]
    cosine = jnp.cos(angles)[:, None, :]
    sine = jnp.sin(angles)[:, None, :]
    first = values[..., :half_width]
    second = values[..., half_width:]
    return jnp.concatenate([first * cosine - second * sine, second * cosine + first * sine], axis=-1)


def attend_row(inputs):
    query, key_new, value_new, key_rows, value_rows, length = inputs
    kv_heads = key_rows.shape[0]
    queries = query.reshape(kv_heads, -1, query.shape[-1]).astype(jnp.float32)
    scale = query.shape[-1] ** -0.5
    scores = jnp.einsum("gqd,gpd->gqp", queries, key_rows.astype(jnp.float32)) * scale
    valid_keys = jnp.arange(key_rows.shape[1])[None, None, :] < length
    scores = jnp.where(valid_keys, scores, -jnp.inf)
    own_score = jnp.einsum("gqd,gd->gq", queries, key_new.astype(jnp.float32)) * scale
    peak = jnp.maximum(jnp.max(scores, axis=-1), own_score)
    exps = jnp.exp(scores - peak[..., None])
    own_exp = jnp.exp(own_score - peak)
    total = jnp.sum(exps, axis=-1) + own_exp
    weights = (exps / total[..., None]).astype(jnp.bfloat16)
    own_weight = (own_exp / total).astype(jnp.bfloat16)
    mixed = jnp.einsum("gqp,gpd->gqd", weights.astype(jnp.float32), value_rows.astype(jnp.float32))
    mixed = mixed + own_weight.astype(jnp.float32)[..., None] * value_new.astype(jnp.float32)[:, None, :]
    return mixed.astype(jnp.bfloat16).reshape(-1)


def reference(tokens, query_weight, key_weight, value_weight, output_weight, key_cache, value_cache, lengths):
    query = jnp.dot(tokens, query_weight.T, preferred_element_type=jnp.float32).astype(jnp.bfloat16)
    key_new = jnp.dot(tokens, key_weight.T, preferred_element_type=jnp.float32).astype(jnp.bfloat16)
    value_new = jnp.dot(tokens, value_weight.T, preferred_element_type=jnp.float32).astype(jnp.bfloat16)
    positions = lengths.astype(jnp.float32)
    query_rot = rotate(query.astype(jnp.float32).reshape(ROWS, HQ, HD), positions).astype(jnp.bfloat16)
    key_rot = rotate(key_new.astype(jnp.float32).reshape(ROWS, KVH, HD), positions).astype(jnp.bfloat16)
    value_heads = value_new.reshape(ROWS, KVH, HD)
    attended = lax.map(attend_row, (query_rot, key_rot, value_heads, key_cache, value_cache, lengths))
    return jnp.dot(attended, output_weight.T, preferred_element_type=jnp.float32).astype(jnp.bfloat16)
```

```python
import math

import jax
import jax.numpy as jnp
from jax import lax
from jax.experimental import pallas as pl
from jax.experimental.pallas import tpu as pltpu
from jax.sharding import PartitionSpec as P

HD = 128
HQ = 96
KVH = 6
MESH = pl.DeviceIdType.MESH
NT = (((1,), (1,)), ((), ()))

GX = 8
TOK_ROWS = 128
Q_CHUNK = 256
O_CHUNK = 256


def gather_start(buf, size, z, x, send, recv):
    me = 2 * z + x
    slot = buf.at[pl.ds(pl.multiple_of(me * size, size), size)]
    copies = []
    for d in (2, 1, 3):
        copies.append(
            pltpu.make_async_remote_copy(
                slot, slot, send.at[d - 1], recv.at[me],
                device_id={"gx": 2 * lax.rem(z + d, 4) + x}, device_id_type=MESH,
            )
        )
    copies.append(
        pltpu.make_async_remote_copy(
            slot, slot, send.at[3], recv.at[me],
            device_id={"gx": 2 * z + 1 - x}, device_id_type=MESH,
        )
    )
    for copy in copies:
        copy.start()
    return copies


def gather_finish(buf, size, z, x, send, recv):
    other = 2 * z + 1 - x

    def piece(s):
        return buf.at[pl.ds(pl.multiple_of(s * size, size), size)]

    copies = []
    for d in (1, 3, 2):
        s = 2 * lax.rem(z + d, 4) + x
        copy = pltpu.make_async_remote_copy(
            piece(s), piece(s), send.at[3 + d], recv.at[s],
            device_id={"gx": other}, device_id_type=MESH,
        )
        copy.wait_recv()
        copy.start()
        copies.append(copy)
    for d in range(4):
        s = 2 * lax.rem(z + d, 4) + 1 - x
        pltpu.make_async_remote_copy(
            piece(s), piece(s), send.at[3], recv.at[s],
            device_id={"gx": other}, device_id_type=MESH,
        ).wait_recv()
    return copies


def kernel(
    len_ref, tok_ref, wq_hbm, wk_hbm, wv_hbm, wo_hbm, kc_hbm, vc_hbm, out_ref,
    wq, wkv, wo, kc, vc, tok_f, xr, xf, xb, part, other_part, summed, got, qs, ag, agf, ab,
    terms, other_terms,
    wq_sem, wkv_sem, wo_sem, c_sem, x_send, x_recv, p_send, p_recv, m_send, m_recv,
    a_send, a_recv, t_send, t_recv,
):
    i = lax.axis_index("gx")
    c = lax.axis_index("gy")
    z, x = i // 2, lax.rem(i, 2)
    half = i // 4
    n_q, n_o = wq.shape[0], wo.shape[0]
    kw = wk_hbm.shape[0]

    def wq_copy(t):
        return pltpu.make_async_copy(wq_hbm.at[pl.ds(pl.multiple_of(t * Q_CHUNK, Q_CHUNK), Q_CHUNK)], wq.at[t], wq_sem.at[t])

    def wo_copy(t):
        return pltpu.make_async_copy(wo_hbm.at[pl.ds(pl.multiple_of(t * O_CHUNK, O_CHUNK), O_CHUNK)], wo.at[t], wo_sem.at[t])

    wk_copy = pltpu.make_async_copy(wk_hbm, wkv.at[pl.ds(0, kw)], wkv_sem.at[0])
    wv_copy = pltpu.make_async_copy(wv_hbm, wkv.at[pl.ds(128, kw)], wkv_sem.at[1])
    wk_copy.start()
    wv_copy.start()
    for t in range(n_q):
        wq_copy(t).start()
    kc_copy = pltpu.make_async_copy(kc_hbm, kc, c_sem.at[0])
    vc_copy = pltpu.make_async_copy(vc_hbm, vc, c_sem.at[1])
    kc_copy.start()
    vc_copy.start()

    barrier = pltpu.get_barrier_semaphore()
    for o in range(1, 2 * GX):
        at = lax.rem(i * 2 + c + o, 2 * GX)
        pl.semaphore_signal(
            barrier, inc=1, device_id={"gx": at // 2, "gy": lax.rem(at, 2)}, device_id_type=MESH
        )
    tok = tok_ref[...].astype(jnp.float32)
    pieces = tok.shape[1] // HD
    for k in range(pieces):
        tok_f[pl.ds(k, 2, stride=pieces), :] = tok[:, k * HD : (k + 1) * HD]
    xr[pl.ds(pl.multiple_of(i * TOK_ROWS, TOK_ROWS), TOK_ROWS), :] = tok_f[...].astype(jnp.bfloat16)
    pl.semaphore_wait(barrier, 2 * GX - 1)

    sends = gather_start(xr, TOK_ROWS, z, x, x_send, x_recv)
    wkv[kw:128, :] = jnp.zeros((128 - kw, wkv.shape[1]), jnp.bfloat16)
    wkv[128 + kw : 256, :] = jnp.zeros((128 - kw, wkv.shape[1]), jnp.bfloat16)
    lane = lax.broadcasted_iota(jnp.int32, (8, HD), 1)
    row_id = lax.broadcasted_iota(jnp.int32, (8, HD), 0)
    index = lax.rem(lane, HD // 2).astype(jnp.float32)
    freqs = jnp.exp(-(index * (2.0 / HD)) * math.log(500000.0))
    lengths = jnp.where(row_id == 0, len_ref[0], len_ref[1])
    angles = lengths.astype(jnp.float32) * freqs
    cosine = jnp.cos(angles)
    sine = jnp.sin(angles)
    sine = jnp.where(lane < HD // 2, -sine, sine)
    sends += gather_finish(xr, TOK_ROWS, z, x, x_send, x_recv)

    xf[...] = xr[...].astype(jnp.float32)
    for k in range(pieces):
        xb[:, k * HD : (k + 1) * HD] = xf[pl.ds(k, 16, stride=pieces), :].astype(jnp.bfloat16)

    def put(h, value):
        part[pl.ds(h, 16, stride=16), :] = value

    wk_copy.wait()
    wv_copy.wait()
    kv = lax.dot_general(xb[...], wkv[...], NT, preferred_element_type=jnp.float32)
    put(12, kv[:, :128])
    put(13, kv[:, 128:])
    put(14, jnp.zeros((16, 128), jnp.float32))
    put(15, jnp.zeros((16, 128), jnp.float32))

    heads = Q_CHUNK // HD

    @pl.loop(0, n_q)
    def _(t):
        wq_copy(t).wait()
        wo_copy(t).start()
        value = lax.dot_general(xb[...], wq[t], NT, preferred_element_type=jnp.float32)
        for e in range(heads):
            put(t * heads + e, value[:, e * HD : (e + 1) * HD])

    for t in range(n_q, n_o):
        wo_copy(t).start()

    away = pltpu.make_async_remote_copy(
        part.at[pl.ds(pl.multiple_of((1 - c) * 128, 128), 128)], other_part, p_send.at[0], p_recv.at[0],
        device_id={"gy": 1 - c}, device_id_type=MESH,
    )
    away.start()
    away.wait_recv()
    summed[...] = (part[pl.ds(pl.multiple_of(c * 128, 128), 128), :] + other_part[...]).astype(jnp.bfloat16)

    mine = lax.rem(i, 4)

    def message(o):
        return pltpu.make_async_remote_copy(
            summed.at[pl.ds(o * 32, 32)], got.at[pl.ds(pl.multiple_of(mine * 32, 32), 32)],
            m_send.at[o], m_recv.at[mine],
            device_id={"gx": 4 * c + o, "gy": half}, device_id_type=MESH,
        )

    def message_here(o):
        return pltpu.make_async_copy(
            summed.at[pl.ds(o * 32, 32)], got.at[pl.ds(o * 32, 32)], m_recv.at[o]
        )

    for o in range(4):
        itself = jnp.logical_and(c == half, mine == o)

        @pl.when(itself)
        def _():
            message_here(o).start()

        @pl.when(jnp.logical_not(itself))
        def _():
            message(o).start()

    kc_copy.wait()
    vc_copy.wait()
    for s in range(4):
        message_here(s).wait()
    scale = HD ** (-0.5)
    for r in range(2):
        keys, values = [], []
        for s in range(4):
            block = got[s * 32 + r * 16 : s * 32 + r * 16 + 16, :].astype(jnp.float32)
            qs[r * 48 + 12 * s : r * 48 + 12 * s + 12, :] = block[0:12, :]
            keys.append(block[12:13, :kw])
            values.append(block[13:14, :kw])
        keys = jnp.concatenate(keys, axis=1)
        values = jnp.concatenate(values, axis=1)
        cos_r = cosine[r : r + 1, :]
        sin_r = sine[r : r + 1, :]
        for g in range(3):
            k_new = keys[:, g * HD : (g + 1) * HD]
            v_new = values[:, g * HD : (g + 1) * HD]
            k_rot = (k_new * cos_r + pltpu.roll(k_new, HD // 2, 1) * sin_r).astype(jnp.bfloat16)
            q = qs[r * 48 + 16 * g : r * 48 + 16 * g + 16, :]
            q_rot = (q * cos_r + pltpu.roll(q, HD // 2, 1) * sin_r).astype(jnp.bfloat16)
            own = jnp.sum(
                q_rot.astype(jnp.float32) * k_rot.astype(jnp.float32), axis=1, keepdims=True
            ) * scale
            scores = lax.dot_general(
                q_rot, kc[r, g], NT, preferred_element_type=jnp.float32
            ) * scale
            position = lax.broadcasted_iota(jnp.int32, scores.shape, 1)
            scores = jnp.where(position < len_ref[r], scores, -jnp.inf)
            peak = jnp.maximum(jnp.max(scores, axis=1, keepdims=True), own)
            exps = jnp.exp(scores - peak)
            own_exp = jnp.exp(own - peak)
            total = jnp.sum(exps, axis=1, keepdims=True) + own_exp
            weights = (exps / total).astype(jnp.bfloat16)
            own_weight = (own_exp / total).astype(jnp.bfloat16).astype(jnp.float32)
            mixed = jnp.dot(weights, vc[r, g], preferred_element_type=jnp.float32)
            mixed = mixed + own_weight * v_new
            ag[pl.ds(pl.multiple_of(i * 96 + r * 48 + 16 * g, 16), 16), :] = mixed.astype(jnp.bfloat16)

    sends += gather_start(ag, 96, z, x, a_send, a_recv)
    sends += gather_finish(ag, 96, z, x, a_send, a_recv)
    agf[...] = ag[...].astype(jnp.float32)
    for h in range(48):
        ab[:, h * HD : (h + 1) * HD] = agf[pl.ds(h, 16, stride=48), :].astype(jnp.bfloat16)

    theirs = pl.multiple_of((1 - c) * 8, 8)
    ours = pl.multiple_of(c * 8, 8)

    def term_copy(t):
        return pltpu.make_async_remote_copy(
            terms.at[t, pl.ds(theirs, 8)], other_terms.at[t], t_send.at[t], t_recv.at[t],
            device_id={"gy": 1 - c}, device_id_type=MESH,
        )

    @pl.loop(0, n_o)
    def _(t):
        wo_copy(t).wait()
        terms[t] = lax.dot_general(ab[...], wo[t], NT, preferred_element_type=jnp.float32)
        term_copy(t).start()

    for t in range(n_o):
        term_copy(t).wait_recv()
        out_ref[:, t * O_CHUNK : (t + 1) * O_CHUNK] = (
            terms[t, pl.ds(ours, 8), :] + other_terms[t]
        ).astype(jnp.bfloat16)

    for copy in sends:
        copy.wait_send()
    away.wait_send()
    for t in range(n_o):
        term_copy(t).wait_send()
    for o in range(4):
        itself = jnp.logical_and(c == half, mine == o)

        @pl.when(jnp.logical_not(itself))
        def _():
            message(o).wait_send()


def fused(tokens, query_weight, key_weight, value_weight, output_weight, key_cache, value_cache, lengths):
    depth = tokens.shape[1]
    n_q = query_weight.shape[0] // Q_CHUNK
    n_o = output_weight.shape[0] // O_CHUNK
    head_w = output_weight.shape[1]
    anywhere = pl.BlockSpec(memory_space=pl.ANY)
    in_vmem = pl.BlockSpec(memory_space=pltpu.VMEM)
    f32, bf16, dma = jnp.float32, jnp.bfloat16, pltpu.SemaphoreType.DMA
    return pl.pallas_call(
        kernel,
        out_shape=jax.ShapeDtypeStruct((GX, output_weight.shape[0]), bf16),
        in_specs=[pl.BlockSpec(memory_space=pltpu.SMEM), in_vmem] + [anywhere] * 6,
        out_specs=in_vmem,
        scratch_shapes=[
            pltpu.VMEM((n_q, Q_CHUNK, depth), bf16),
            pltpu.VMEM((256, depth), bf16),
            pltpu.VMEM((n_o, O_CHUNK, head_w), bf16),
            pltpu.VMEM(key_cache.shape, bf16),
            pltpu.VMEM(value_cache.shape, bf16),
            pltpu.VMEM((TOK_ROWS, HD), f32),
            pltpu.VMEM((GX * TOK_ROWS, HD), bf16),
            pltpu.VMEM((GX * TOK_ROWS, HD), f32),
            pltpu.VMEM((16, depth), bf16),
            pltpu.VMEM((256, 128), f32),
            pltpu.VMEM((128, 128), f32),
            pltpu.VMEM((128, 128), bf16),
            pltpu.VMEM((128, 128), bf16),
            pltpu.VMEM((96, 128), f32),
            pltpu.VMEM((GX * 96, 128), bf16),
            pltpu.VMEM((GX * 96, 128), f32),
            pltpu.VMEM((16, head_w), bf16),
            pltpu.VMEM((n_o, 16, O_CHUNK), f32),
            pltpu.VMEM((n_o, 8, O_CHUNK), f32),
            dma((n_q,)), dma((2,)), dma((n_o,)), dma((2,)),
            dma((7,)), dma((GX,)), dma((1,)), dma((1,)), dma((4,)), dma((4,)),
            dma((7,)), dma((GX,)), dma((n_o,)), dma((n_o,)),
        ],
        compiler_params=pltpu.CompilerParams(
            collective_id=0, has_side_effects=True, vmem_limit_bytes=60 * 2**20
        ),
        cost_estimate=pl.CostEstimate(
            flops=1 << 30, bytes_accessed=54 << 20, transcendentals=1 << 15
        ),
    )(lengths, tokens, query_weight, key_weight, value_weight, output_weight, key_cache, value_cache)


def fits_fused(tokens, query_weight, key_weight, output_weight, key_cache):
    return (
        lax.axis_size("gx") == GX
        and lax.axis_size("gy") == 2
        and tokens.shape == (2, TOK_ROWS * HD // 2)
        and query_weight.shape[0] == 12 * HD
        and key_weight.shape[0] == 96
        and key_cache.shape == (2, 3, 256, HD)
        and output_weight.shape == (2048, 48 * HD)
    )


def rotate(values, positions):
    half_width = values.shape[-1] // 2
    freqs = jnp.exp(
        -(jnp.arange(half_width, dtype=jnp.float32) * (2.0 / values.shape[-1])) * math.log(500000.0)
    )
    angles = positions[:, None] * freqs[None, :]
    cosine = jnp.cos(angles)[:, None, :]
    sine = jnp.sin(angles)[:, None, :]
    first = values[..., :half_width]
    second = values[..., half_width:]
    return jnp.concatenate(
        [first * cosine - second * sine, second * cosine + first * sine], axis=-1
    )


def product(row_piece, matrix):
    return lax.dot_general(
        row_piece, matrix, (((1,), (1,)), ((), ())), preferred_element_type=jnp.float32
    )


def local(
    tokens, query_weight, key_weight, value_weight, output_weight, key_cache, value_cache, lengths
):
    if fits_fused(tokens, query_weight, key_weight, output_weight, key_cache):
        return fused(
            tokens, query_weight, key_weight, value_weight, output_weight, key_cache, value_cache, lengths
        )
    rows_here = tokens.shape[0]
    width_gx = lax.axis_size("gx")
    width_query = query_weight.shape[0]
    width_key = key_weight.shape[0]
    width_all = width_query + 2 * width_key
    local_heads = key_cache.shape[1]
    group_size = HQ // KVH
    row_piece = lax.all_gather(tokens, "gx", axis=0, tiled=True)
    partial_value = jnp.concatenate(
        [
            product(row_piece, query_weight),
            product(row_piece, key_weight),
            product(row_piece, value_weight),
        ],
        axis=1,
    )
    summed = lax.psum(partial_value, "gy").astype(jnp.bfloat16)
    owned = lax.all_to_all(summed, "gx", split_axis=0, concat_axis=1, tiled=True)
    blocks = owned.reshape(rows_here, width_gx, width_all)
    query_all = blocks[:, :, :width_query].reshape(rows_here, HQ, HD)
    key_all = blocks[:, :, width_query : width_query + width_key].reshape(rows_here, KVH, HD)
    value_all = blocks[:, :, width_query + width_key :].reshape(rows_here, KVH, HD)
    shard = lax.axis_index("gy")
    query_part = lax.dynamic_slice_in_dim(
        query_all, shard * local_heads * group_size, local_heads * group_size, 1
    )
    key_part = lax.dynamic_slice_in_dim(key_all, shard * local_heads, local_heads, 1)
    value_part = lax.dynamic_slice_in_dim(value_all, shard * local_heads, local_heads, 1)
    positions = lengths.astype(jnp.float32)
    query_rot = rotate(query_part.astype(jnp.float32), positions).astype(jnp.bfloat16)
    query_rot = query_rot.reshape(rows_here, local_heads, group_size, HD)
    key_rot = rotate(key_part.astype(jnp.float32), positions).astype(jnp.bfloat16)
    scale = HD ** (-0.5)
    own_score = (
        jnp.einsum("rgqd,rgd->rgq", query_rot, key_rot, preferred_element_type=jnp.float32) * scale
    )
    cache_len = key_cache.shape[2]
    scores = (
        jnp.einsum("rgqd,rgpd->rgqp", query_rot, key_cache, preferred_element_type=jnp.float32)
        * scale
    )
    valid_keys = jnp.arange(cache_len)[None, None, None, :] < lengths[:, None, None, None]
    scores = jnp.where(valid_keys, scores, -jnp.inf)
    peak = jnp.maximum(jnp.max(scores, axis=-1), own_score)
    exps = jnp.exp(scores - peak[..., None])
    own_exp = jnp.exp(own_score - peak)
    total = jnp.sum(exps, axis=-1) + own_exp
    weights = (exps / total[..., None]).astype(jnp.bfloat16)
    mixed = jnp.einsum("rgqp,rgpd->rgqd", weights, value_cache, preferred_element_type=jnp.float32)
    own_weight = (own_exp / total).astype(jnp.bfloat16)
    mixed = (
        mixed
        + own_weight.astype(jnp.float32)[..., None] * value_part.astype(jnp.float32)[:, :, None, :]
    )
    attended = mixed.astype(jnp.bfloat16).reshape(rows_here, local_heads * group_size * HD)
    terms = product(lax.all_gather(attended, "gx", axis=0, tiled=True), output_weight)
    return lax.psum_scatter(terms, "gy", scatter_dimension=0, tiled=True).astype(jnp.bfloat16)


def solution(mesh):
    in_specs = (
        P(("groups", "gx"), "gy"),
        P("gx", "gy"),
        P("gx", "gy"),
        P("gx", "gy"),
        P("gx", "gy"),
        P(("groups", "gx"), "gy", None, None),
        P(("groups", "gx"), "gy", None, None),
        P(("groups", "gx")),
    )
    out_specs = P(("groups", "gy"), "gx")
    return jax.shard_map(local, mesh=mesh, in_specs=in_specs, out_specs=out_specs, check_vma=False)
```

```python
import math

import jax
import jax.numpy as jnp
from jax import lax
from jax.experimental import pallas as pl
from jax.experimental.pallas import tpu as pltpu
from jax.sharding import PartitionSpec as P

HD = 128
HQ = 96
KVH = 6
MESH = pl.DeviceIdType.MESH
NT = (((1,), (1,)), ((), ()))

GX = 8
TOK_ROWS = 128
Q_CHUNK = 512
O_CHUNK = 512


class Gather:
    def __init__(self, buf, base, size, z, x, send, recv, n):
        self.buf, self.base, self.size, self.z, self.x = buf, base, size, z, x
        self.send, self.recv, self.n = send, recv, n

    def slot_at(self, d, x):
        return 2 * lax.rem(self.z + d, 4) + x

    def copy(self, slot, sem, to):
        rows = pl.ds(pl.multiple_of(self.base + slot * self.size, self.size), self.size)
        block = self.buf.at[rows]
        return pltpu.make_async_remote_copy(
            block, block, self.send.at[7 * self.n + sem], self.recv.at[GX * self.n + slot],
            device_id={"gx": to}, device_id_type=MESH,
        )

    def start(self):
        me, over = self.slot_at(0, self.x), self.slot_at(0, 1 - self.x)
        copies = [self.copy(me, d - 1, self.slot_at(d, self.x)) for d in (2, 1, 3)]
        copies.append(self.copy(me, 3, over))
        for copy in copies:
            copy.start()
        return copies

    def forward(self):
        over = self.slot_at(0, 1 - self.x)
        copies = [self.copy(self.slot_at(d, self.x), 3 + d, over) for d in (1, 3, 2)]
        for copy in copies:
            copy.wait_recv()
            copy.start()
        return copies

    def wait(self):
        over = self.slot_at(0, 1 - self.x)
        for d in range(4):
            self.copy(self.slot_at(d, 1 - self.x), 3, over).wait_recv()


def kernel(
    len_ref, tok_ref, wq_hbm, wk_hbm, wv_hbm, wo_hbm, kc_hbm, vc_hbm, out_ref,
    wq, wkv, wo, kc, vc, tok_f, xr, xf, xb, part, other_part, summed, got, qs, ag, agf, ab,
    terms, other_terms,
    wq_sem, wkv_sem, wo_sem, c_sem, x_send, x_recv, p_send, p_recv, m_send, m_recv,
    a_send, a_recv, t_send, t_recv,
):
    i = lax.axis_index("gx")
    c = lax.axis_index("gy")
    z, x = i // 2, lax.rem(i, 2)
    half = i // 4
    n_q, n_o = wq.shape[0], wo.shape[0]
    kw = wk_hbm.shape[0]

    def wq_copy(t):
        return pltpu.make_async_copy(wq_hbm.at[pl.ds(pl.multiple_of(t * Q_CHUNK, Q_CHUNK), Q_CHUNK)], wq.at[t], wq_sem.at[t])

    def wo_copy(t):
        return pltpu.make_async_copy(wo_hbm.at[pl.ds(pl.multiple_of(t * O_CHUNK, O_CHUNK), O_CHUNK)], wo.at[t], wo_sem.at[t])

    wk_copy = pltpu.make_async_copy(wk_hbm, wkv.at[pl.ds(0, kw)], wkv_sem.at[0])
    wv_copy = pltpu.make_async_copy(wv_hbm, wkv.at[pl.ds(128, kw)], wkv_sem.at[1])
    wk_copy.start()
    wv_copy.start()
    for t in range(n_q):
        wq_copy(t).start()
    kc_copy = pltpu.make_async_copy(kc_hbm, kc, c_sem.at[0])
    vc_copy = pltpu.make_async_copy(vc_hbm, vc, c_sem.at[1])
    kc_copy.start()
    vc_copy.start()

    barrier = pltpu.get_barrier_semaphore()
    def greet(gx, gy):
        pl.semaphore_signal(barrier, inc=1, device_id={"gx": gx, "gy": gy}, device_id_type=MESH)

    mine = lax.rem(i, 4)
    greet(i, 1 - c)
    greet(2 * z + 1 - x, c)
    for d in range(1, 4):
        greet(2 * lax.rem(z + d, 4) + x, c)
    for o in range(4):

        @pl.when(jnp.logical_not(jnp.logical_and(c == half, mine == o)))
        def _():
            greet(4 * c + o, half)

    tok = tok_ref[...].astype(jnp.float32)
    pieces = tok.shape[1] // HD
    for k in range(pieces):
        tok_f[pl.ds(k, 2, stride=pieces), :] = tok[:, k * HD : (k + 1) * HD]
    xr[pl.ds(pl.multiple_of(i * TOK_ROWS, TOK_ROWS), TOK_ROWS), :] = tok_f[...].astype(jnp.bfloat16)

    @pl.when(c == half)
    def _():
        pl.semaphore_wait(barrier, 8)

    @pl.when(c != half)
    def _():
        pl.semaphore_wait(barrier, 9)


    tok_gather = Gather(xr, 0, TOK_ROWS, z, x, x_send, x_recv, 0)
    sends = tok_gather.start()
    wkv[kw:128, :] = jnp.zeros((128 - kw, wkv.shape[1]), jnp.bfloat16)
    wkv[128 + kw : 256, :] = jnp.zeros((128 - kw, wkv.shape[1]), jnp.bfloat16)
    lane = lax.broadcasted_iota(jnp.int32, (8, HD), 1)
    row_id = lax.broadcasted_iota(jnp.int32, (8, HD), 0)
    index = lax.rem(lane, HD // 2).astype(jnp.float32)
    freqs = jnp.exp(-(index * (2.0 / HD)) * math.log(500000.0))
    lengths = jnp.where(row_id == 0, len_ref[0], len_ref[1])
    angles = lengths.astype(jnp.float32) * freqs
    cosine = jnp.cos(angles)
    sine = jnp.sin(angles)
    sine = jnp.where(lane < HD // 2, -sine, sine)
    sends += tok_gather.forward()
    tok_gather.wait()

    xf[...] = xr[...].astype(jnp.float32)
    for k in range(pieces):
        xb[:, k * HD : (k + 1) * HD] = xf[pl.ds(k, 16, stride=pieces), :].astype(jnp.bfloat16)

    def put(h, value):
        part[pl.ds(h, 16, stride=16), :] = value

    wk_copy.wait()
    wv_copy.wait()
    kv = lax.dot_general(xb[...], wkv[...], NT, preferred_element_type=jnp.float32)
    put(12, kv[:, :128])
    put(13, kv[:, 128:])
    put(14, jnp.zeros((16, 128), jnp.float32))
    put(15, jnp.zeros((16, 128), jnp.float32))

    heads = Q_CHUNK // HD

    @pl.loop(0, n_q)
    def _(t):
        wq_copy(t).wait()
        wo_copy(t).start()
        value = lax.dot_general(xb[...], wq[t], NT, preferred_element_type=jnp.float32)
        for e in range(heads):
            put(t * heads + e, value[:, e * HD : (e + 1) * HD])

    for t in range(n_q, n_o):
        wo_copy(t).start()

    away = pltpu.make_async_remote_copy(
        part.at[pl.ds(pl.multiple_of((1 - c) * 128, 128), 128)], other_part, p_send.at[0], p_recv.at[0],
        device_id={"gy": 1 - c}, device_id_type=MESH,
    )
    away.start()
    away.wait_recv()
    summed[...] = (part[pl.ds(pl.multiple_of(c * 128, 128), 128), :] + other_part[...]).astype(jnp.bfloat16)

    def message(o):
        return pltpu.make_async_remote_copy(
            summed.at[pl.ds(o * 32, 32)], got.at[pl.ds(pl.multiple_of(mine * 32, 32), 32)],
            m_send.at[o], m_recv.at[mine],
            device_id={"gx": 4 * c + o, "gy": half}, device_id_type=MESH,
        )

    def message_here(o):
        return pltpu.make_async_copy(
            summed.at[pl.ds(o * 32, 32)], got.at[pl.ds(o * 32, 32)], m_recv.at[o]
        )

    for o in range(4):
        itself = jnp.logical_and(c == half, mine == o)

        @pl.when(itself)
        def _():
            message_here(o).start()

        @pl.when(jnp.logical_not(itself))
        def _():
            message(o).start()

    kc_copy.wait()
    vc_copy.wait()
    for s in range(4):
        message_here(s).wait()
    scale = HD ** (-0.5)
    rows = []
    for r in range(2):
        keys, values = [], []
        for s in range(4):
            block = got[s * 32 + r * 16 : s * 32 + r * 16 + 16, :].astype(jnp.float32)
            qs[r * 48 + 12 * s : r * 48 + 12 * s + 12, :] = block[0:12, :]
            keys.append(block[12:13, :kw])
            values.append(block[13:14, :kw])
        rows.append((jnp.concatenate(keys, axis=1), jnp.concatenate(values, axis=1)))
    gathers = []
    for g in range(3):
        for r in range(2):
            keys, values = rows[r]
            cos_r = cosine[r : r + 1, :]
            sin_r = sine[r : r + 1, :]
            k_new = keys[:, g * HD : (g + 1) * HD]
            v_new = values[:, g * HD : (g + 1) * HD]
            k_rot = (k_new * cos_r + pltpu.roll(k_new, HD // 2, 1) * sin_r).astype(jnp.bfloat16)
            q = qs[r * 48 + 16 * g : r * 48 + 16 * g + 16, :]
            q_rot = (q * cos_r + pltpu.roll(q, HD // 2, 1) * sin_r).astype(jnp.bfloat16)
            own = jnp.sum(
                q_rot.astype(jnp.float32) * k_rot.astype(jnp.float32), axis=1, keepdims=True
            ) * scale
            scores = lax.dot_general(
                q_rot, kc[r, g], NT, preferred_element_type=jnp.float32
            ) * scale
            position = lax.broadcasted_iota(jnp.int32, scores.shape, 1)
            scores = jnp.where(position < len_ref[r], scores, -jnp.inf)
            peak = jnp.maximum(jnp.max(scores, axis=1, keepdims=True), own)
            exps = jnp.exp(scores - peak)
            own_exp = jnp.exp(own - peak)
            total = jnp.sum(exps, axis=1, keepdims=True) + own_exp
            weights = (exps / total).astype(jnp.bfloat16)
            own_weight = (own_exp / total).astype(jnp.bfloat16).astype(jnp.float32)
            mixed = jnp.dot(weights, vc[r, g], preferred_element_type=jnp.float32)
            mixed = mixed + own_weight * v_new
            ag[pl.ds(pl.multiple_of(g * 256 + i * 32 + r * 16, 16), 16), :] = mixed.astype(jnp.bfloat16)
        gathers.append(Gather(ag, g * 256, 32, z, x, a_send, a_recv, g))
        sends += gathers[g].start()
    for gather in gathers:
        sends += gather.forward()

    theirs = pl.multiple_of((1 - c) * 8, 8)
    ours = pl.multiple_of(c * 8, 8)

    def term_copy(t):
        return pltpu.make_async_remote_copy(
            terms.at[t, pl.ds(theirs, 8)], other_terms.at[t], t_send.at[t], t_recv.at[t],
            device_id={"gy": 1 - c}, device_id_type=MESH,
        )

    width = 16 * HD
    for g in range(3):
        gathers[g].wait()
        agf[...] = ag[g * 256 : (g + 1) * 256, :].astype(jnp.float32)
        for h in range(16):
            ab[:, h * HD : (h + 1) * HD] = agf[pl.ds(h, 16, stride=16), :].astype(jnp.bfloat16)

        @pl.loop(0, n_o)
        def _(t):
            if g == 0:
                wo_copy(t).wait()
            value = lax.dot_general(
                ab[...], wo[t, :, g * width : (g + 1) * width], NT, preferred_element_type=jnp.float32
            )
            terms[t] = value if g == 0 else terms[t] + value
            if g == 2:
                term_copy(t).start()

    for t in range(n_o):
        term_copy(t).wait_recv()
        out_ref[:, t * O_CHUNK : (t + 1) * O_CHUNK] = (
            terms[t, pl.ds(ours, 8), :] + other_terms[t]
        ).astype(jnp.bfloat16)

    for copy in sends:
        copy.wait_send()
    away.wait_send()
    for t in range(n_o):
        term_copy(t).wait_send()
    for o in range(4):
        itself = jnp.logical_and(c == half, mine == o)

        @pl.when(jnp.logical_not(itself))
        def _():
            message(o).wait_send()


def fused(tokens, query_weight, key_weight, value_weight, output_weight, key_cache, value_cache, lengths):
    depth = tokens.shape[1]
    n_q = query_weight.shape[0] // Q_CHUNK
    n_o = output_weight.shape[0] // O_CHUNK
    head_w = output_weight.shape[1]
    anywhere = pl.BlockSpec(memory_space=pl.ANY)
    in_vmem = pl.BlockSpec(memory_space=pltpu.VMEM)
    f32, bf16, dma = jnp.float32, jnp.bfloat16, pltpu.SemaphoreType.DMA
    return pl.pallas_call(
        kernel,
        out_shape=jax.ShapeDtypeStruct((GX, output_weight.shape[0]), bf16),
        in_specs=[pl.BlockSpec(memory_space=pltpu.SMEM), in_vmem] + [anywhere] * 6,
        out_specs=in_vmem,
        scratch_shapes=[
            pltpu.VMEM((n_q, Q_CHUNK, depth), bf16),
            pltpu.VMEM((256, depth), bf16),
            pltpu.VMEM((n_o, O_CHUNK, head_w), bf16),
            pltpu.VMEM(key_cache.shape, bf16),
            pltpu.VMEM(value_cache.shape, bf16),
            pltpu.VMEM((TOK_ROWS, HD), f32),
            pltpu.VMEM((GX * TOK_ROWS, HD), bf16),
            pltpu.VMEM((GX * TOK_ROWS, HD), f32),
            pltpu.VMEM((16, depth), bf16),
            pltpu.VMEM((256, 128), f32),
            pltpu.VMEM((128, 128), f32),
            pltpu.VMEM((128, 128), bf16),
            pltpu.VMEM((128, 128), bf16),
            pltpu.VMEM((96, 128), f32),
            pltpu.VMEM((GX * 96, 128), bf16),
            pltpu.VMEM((GX * 32, 128), f32),
            pltpu.VMEM((16, 16 * HD), bf16),
            pltpu.VMEM((n_o, 16, O_CHUNK), f32),
            pltpu.VMEM((n_o, 8, O_CHUNK), f32),
            dma((n_q,)), dma((2,)), dma((n_o,)), dma((2,)),
            dma((7,)), dma((GX,)), dma((1,)), dma((1,)), dma((4,)), dma((4,)),
            dma((21,)), dma((3 * GX,)), dma((n_o,)), dma((n_o,)),
        ],
        compiler_params=pltpu.CompilerParams(
            collective_id=0, has_side_effects=True, vmem_limit_bytes=60 * 2**20
        ),
        cost_estimate=pl.CostEstimate(
            flops=1 << 30, bytes_accessed=54 << 20, transcendentals=1 << 15
        ),
    )(lengths, tokens, query_weight, key_weight, value_weight, output_weight, key_cache, value_cache)


def fits_fused(tokens, query_weight, key_weight, output_weight, key_cache):
    return (
        lax.axis_size("gx") == GX
        and lax.axis_size("gy") == 2
        and tokens.shape == (2, TOK_ROWS * HD // 2)
        and query_weight.shape[0] == 12 * HD
        and key_weight.shape[0] == 96
        and key_cache.shape == (2, 3, 256, HD)
        and output_weight.shape == (2048, 48 * HD)
    )


def rotate(values, positions):
    half_width = values.shape[-1] // 2
    freqs = jnp.exp(
        -(jnp.arange(half_width, dtype=jnp.float32) * (2.0 / values.shape[-1])) * math.log(500000.0)
    )
    angles = positions[:, None] * freqs[None, :]
    cosine = jnp.cos(angles)[:, None, :]
    sine = jnp.sin(angles)[:, None, :]
    first = values[..., :half_width]
    second = values[..., half_width:]
    return jnp.concatenate(
        [first * cosine - second * sine, second * cosine + first * sine], axis=-1
    )


def product(row_piece, matrix):
    return lax.dot_general(
        row_piece, matrix, (((1,), (1,)), ((), ())), preferred_element_type=jnp.float32
    )


def local(
    tokens, query_weight, key_weight, value_weight, output_weight, key_cache, value_cache, lengths
):
    if fits_fused(tokens, query_weight, key_weight, output_weight, key_cache):
        return fused(
            tokens, query_weight, key_weight, value_weight, output_weight, key_cache, value_cache, lengths
        )
    rows_here = tokens.shape[0]
    width_gx = lax.axis_size("gx")
    width_query = query_weight.shape[0]
    width_key = key_weight.shape[0]
    width_all = width_query + 2 * width_key
    local_heads = key_cache.shape[1]
    group_size = HQ // KVH
    row_piece = lax.all_gather(tokens, "gx", axis=0, tiled=True)
    partial_value = jnp.concatenate(
        [
            product(row_piece, query_weight),
            product(row_piece, key_weight),
            product(row_piece, value_weight),
        ],
        axis=1,
    )
    summed = lax.psum(partial_value, "gy").astype(jnp.bfloat16)
    owned = lax.all_to_all(summed, "gx", split_axis=0, concat_axis=1, tiled=True)
    blocks = owned.reshape(rows_here, width_gx, width_all)
    query_all = blocks[:, :, :width_query].reshape(rows_here, HQ, HD)
    key_all = blocks[:, :, width_query : width_query + width_key].reshape(rows_here, KVH, HD)
    value_all = blocks[:, :, width_query + width_key :].reshape(rows_here, KVH, HD)
    shard = lax.axis_index("gy")
    query_part = lax.dynamic_slice_in_dim(
        query_all, shard * local_heads * group_size, local_heads * group_size, 1
    )
    key_part = lax.dynamic_slice_in_dim(key_all, shard * local_heads, local_heads, 1)
    value_part = lax.dynamic_slice_in_dim(value_all, shard * local_heads, local_heads, 1)
    positions = lengths.astype(jnp.float32)
    query_rot = rotate(query_part.astype(jnp.float32), positions).astype(jnp.bfloat16)
    query_rot = query_rot.reshape(rows_here, local_heads, group_size, HD)
    key_rot = rotate(key_part.astype(jnp.float32), positions).astype(jnp.bfloat16)
    scale = HD ** (-0.5)
    own_score = (
        jnp.einsum("rgqd,rgd->rgq", query_rot, key_rot, preferred_element_type=jnp.float32) * scale
    )
    cache_len = key_cache.shape[2]
    scores = (
        jnp.einsum("rgqd,rgpd->rgqp", query_rot, key_cache, preferred_element_type=jnp.float32)
        * scale
    )
    valid_keys = jnp.arange(cache_len)[None, None, None, :] < lengths[:, None, None, None]
    scores = jnp.where(valid_keys, scores, -jnp.inf)
    peak = jnp.maximum(jnp.max(scores, axis=-1), own_score)
    exps = jnp.exp(scores - peak[..., None])
    own_exp = jnp.exp(own_score - peak)
    total = jnp.sum(exps, axis=-1) + own_exp
    weights = (exps / total[..., None]).astype(jnp.bfloat16)
    mixed = jnp.einsum("rgqp,rgpd->rgqd", weights, value_cache, preferred_element_type=jnp.float32)
    own_weight = (own_exp / total).astype(jnp.bfloat16)
    mixed = (
        mixed
        + own_weight.astype(jnp.float32)[..., None] * value_part.astype(jnp.float32)[:, :, None, :]
    )
    attended = mixed.astype(jnp.bfloat16).reshape(rows_here, local_heads * group_size * HD)
    terms = product(lax.all_gather(attended, "gx", axis=0, tiled=True), output_weight)
    return lax.psum_scatter(terms, "gy", scatter_dimension=0, tiled=True).astype(jnp.bfloat16)


def solution(mesh):
    in_specs = (
        P(("groups", "gx"), "gy"),
        P("gx", "gy"),
        P("gx", "gy"),
        P("gx", "gy"),
        P("gx", "gy"),
        P(("groups", "gx"), "gy", None, None),
        P(("groups", "gx"), "gy", None, None),
        P(("groups", "gx")),
    )
    out_specs = P(("groups", "gy"), "gx")
    return jax.shard_map(local, mesh=mesh, in_specs=in_specs, out_specs=out_specs, check_vma=False)
```

```python
import math

import jax
import jax.numpy as jnp
from jax import lax
from jax.experimental import pallas as pl
from jax.experimental.pallas import tpu as pltpu
from jax.sharding import PartitionSpec as P

HD = 128
HQ = 96
KVH = 6
MESH = pl.DeviceIdType.MESH
NT = (((1,), (1,)), ((), ()))

GX = 8
TOK_ROWS = 128
Q_CHUNK = 512
O_CHUNK = 512


class Gather:
    def __init__(self, buf, base, size, z, x, send, recv, n):
        self.buf, self.base, self.size, self.z, self.x = buf, base, size, z, x
        self.send, self.recv, self.n = send, recv, n

    def slot_at(self, d, x):
        return 2 * lax.rem(self.z + d, 4) + x

    def copy(self, slot, sem, to):
        rows = pl.ds(pl.multiple_of(self.base + slot * self.size, self.size), self.size)
        block = self.buf.at[rows]
        return pltpu.make_async_remote_copy(
            block, block, self.send.at[7 * self.n + sem], self.recv.at[GX * self.n + slot],
            device_id={"gx": to}, device_id_type=MESH,
        )

    def start(self):
        me, over = self.slot_at(0, self.x), self.slot_at(0, 1 - self.x)
        copies = [self.copy(me, d - 1, self.slot_at(d, self.x)) for d in (2, 1, 3)]
        copies.append(self.copy(me, 3, over))
        for copy in copies:
            copy.start()
        return copies

    def forward(self):
        over = self.slot_at(0, 1 - self.x)
        copies = [self.copy(self.slot_at(d, self.x), 3 + d, over) for d in (1, 3, 2)]
        for copy in copies:
            copy.wait_recv()
            copy.start()
        return copies

    def wait(self):
        over = self.slot_at(0, 1 - self.x)
        for d in range(4):
            self.copy(self.slot_at(d, 1 - self.x), 3, over).wait_recv()


def kernel(
    len_ref, tok_ref, wq_hbm, wk_hbm, wv_hbm, wo_hbm, kc_hbm, vc_hbm, out_ref,
    wq, wkv, wo, kc, vc, tok_f, xr, xf, xb, part, other_part, summed, got, qs, ag, agf, ab,
    terms, other_terms,
    wq_sem, wkv_sem, wo_sem, c_sem, x_send, x_recv, p_send, p_recv, m_send, m_recv,
    a_send, a_recv, t_send, t_recv,
):
    i = lax.axis_index("gx")
    c = lax.axis_index("gy")
    z, x = i // 2, lax.rem(i, 2)
    half = i // 4
    n_q, n_o = wq.shape[0], wo.shape[0]
    kw = wk_hbm.shape[0]

    def wq_copy(t):
        return pltpu.make_async_copy(wq_hbm.at[pl.ds(pl.multiple_of(t * Q_CHUNK, Q_CHUNK), Q_CHUNK)], wq.at[t], wq_sem.at[t])

    def wo_copy(t):
        return pltpu.make_async_copy(wo_hbm.at[pl.ds(pl.multiple_of(t * O_CHUNK, O_CHUNK), O_CHUNK)], wo.at[t], wo_sem.at[t])

    wk_copy = pltpu.make_async_copy(wk_hbm, wkv.at[pl.ds(0, kw)], wkv_sem.at[0])
    wv_copy = pltpu.make_async_copy(wv_hbm, wkv.at[pl.ds(128, kw)], wkv_sem.at[1])
    wk_copy.start()
    wv_copy.start()
    for t in range(n_q):
        wq_copy(t).start()
    kc_copy = pltpu.make_async_copy(kc_hbm, kc, c_sem.at[0])
    vc_copy = pltpu.make_async_copy(vc_hbm, vc, c_sem.at[1])
    kc_copy.start()
    vc_copy.start()

    barrier = pltpu.get_barrier_semaphore()
    def greet(gx, gy):
        pl.semaphore_signal(barrier, inc=1, device_id={"gx": gx, "gy": gy}, device_id_type=MESH)

    mine = lax.rem(i, 4)
    greet(i, 1 - c)
    greet(2 * z + 1 - x, c)
    for d in range(1, 4):
        greet(2 * lax.rem(z + d, 4) + x, c)
    for o in range(4):

        @pl.when(jnp.logical_not(jnp.logical_and(c == half, mine == o)))
        def _():
            greet(4 * c + o, half)

    tok = tok_ref[...].astype(jnp.float32)
    pieces = tok.shape[1] // HD
    for k in range(pieces):
        tok_f[pl.ds(k, 2, stride=pieces), :] = tok[:, k * HD : (k + 1) * HD]
    xr[pl.ds(pl.multiple_of(i * TOK_ROWS, TOK_ROWS), TOK_ROWS), :] = tok_f[...].astype(jnp.bfloat16)

    @pl.when(c == half)
    def _():
        pl.semaphore_wait(barrier, 8)

    @pl.when(c != half)
    def _():
        pl.semaphore_wait(barrier, 9)


    tok_gather = Gather(xr, 0, TOK_ROWS, z, x, x_send, x_recv, 0)
    sends = tok_gather.start()
    wkv[kw:128, :] = jnp.zeros((128 - kw, wkv.shape[1]), jnp.bfloat16)
    wkv[128 + kw : 256, :] = jnp.zeros((128 - kw, wkv.shape[1]), jnp.bfloat16)
    lane = lax.broadcasted_iota(jnp.int32, (8, HD), 1)
    row_id = lax.broadcasted_iota(jnp.int32, (8, HD), 0)
    index = lax.rem(lane, HD // 2).astype(jnp.float32)
    freqs = jnp.exp(-(index * (2.0 / HD)) * math.log(500000.0))
    lengths = jnp.where(row_id == 0, len_ref[0], len_ref[1])
    angles = lengths.astype(jnp.float32) * freqs
    cosine = jnp.cos(angles)
    sine = jnp.sin(angles)
    sine = jnp.where(lane < HD // 2, -sine, sine)
    sends += tok_gather.forward()
    tok_gather.wait()

    xf[...] = xr[...].astype(jnp.float32)
    for k in range(pieces):
        xb[:, k * HD : (k + 1) * HD] = xf[pl.ds(k, 16, stride=pieces), :].astype(jnp.bfloat16)

    def put(h, value):
        part[pl.ds(h, 16, stride=16), :] = value

    wk_copy.wait()
    wv_copy.wait()
    kv = lax.dot_general(xb[...], wkv[...], NT, preferred_element_type=jnp.float32)
    put(12, kv[:, :128])
    put(13, kv[:, 128:])
    put(14, jnp.zeros((16, 128), jnp.float32))
    put(15, jnp.zeros((16, 128), jnp.float32))

    heads = Q_CHUNK // HD

    @pl.loop(0, n_q)
    def _(t):
        wq_copy(t).wait()
        wo_copy(t).start()
        value = lax.dot_general(xb[...], wq[t], NT, preferred_element_type=jnp.float32)
        for e in range(heads):
            put(t * heads + e, value[:, e * HD : (e + 1) * HD])

    for t in range(n_q, n_o):
        wo_copy(t).start()

    away = pltpu.make_async_remote_copy(
        part.at[pl.ds(pl.multiple_of((1 - c) * 128, 128), 128)], other_part, p_send.at[0], p_recv.at[0],
        device_id={"gy": 1 - c}, device_id_type=MESH,
    )
    away.start()
    away.wait_recv()
    summed[...] = (part[pl.ds(pl.multiple_of(c * 128, 128), 128), :] + other_part[...]).astype(jnp.bfloat16)

    def message(o):
        return pltpu.make_async_remote_copy(
            summed.at[pl.ds(o * 32, 32)], got.at[pl.ds(pl.multiple_of(mine * 32, 32), 32)],
            m_send.at[o], m_recv.at[mine],
            device_id={"gx": 4 * c + o, "gy": half}, device_id_type=MESH,
        )

    def message_here(o):
        return pltpu.make_async_copy(
            summed.at[pl.ds(o * 32, 32)], got.at[pl.ds(o * 32, 32)], m_recv.at[o]
        )

    for o in range(4):
        itself = jnp.logical_and(c == half, mine == o)

        @pl.when(itself)
        def _():
            message_here(o).start()

        @pl.when(jnp.logical_not(itself))
        def _():
            message(o).start()

    kc_copy.wait()
    vc_copy.wait()
    for s in range(4):
        message_here(s).wait()
    scale = HD ** (-0.5)
    rows = []
    for r in range(2):
        keys, values = [], []
        for s in range(4):
            block = got[s * 32 + r * 16 : s * 32 + r * 16 + 16, :].astype(jnp.float32)
            qs[r * 48 + 12 * s : r * 48 + 12 * s + 12, :] = block[0:12, :]
            keys.append(block[12:13, :kw])
            values.append(block[13:14, :kw])
        rows.append((jnp.concatenate(keys, axis=1), jnp.concatenate(values, axis=1)))
    gathers = []
    for g in range(3):
        for r in range(2):
            keys, values = rows[r]
            cos_r = cosine[r : r + 1, :]
            sin_r = sine[r : r + 1, :]
            k_new = keys[:, g * HD : (g + 1) * HD]
            v_new = values[:, g * HD : (g + 1) * HD]
            k_rot = (k_new * cos_r + pltpu.roll(k_new, HD // 2, 1) * sin_r).astype(jnp.bfloat16)
            q = qs[r * 48 + 16 * g : r * 48 + 16 * g + 16, :]
            q_rot = (q * cos_r + pltpu.roll(q, HD // 2, 1) * sin_r).astype(jnp.bfloat16)
            own = jnp.sum(
                q_rot.astype(jnp.float32) * k_rot.astype(jnp.float32), axis=1, keepdims=True
            ) * scale
            scores = lax.dot_general(
                q_rot, kc[r, g], NT, preferred_element_type=jnp.float32
            ) * scale
            position = lax.broadcasted_iota(jnp.int32, scores.shape, 1)
            scores = jnp.where(position < len_ref[r], scores, -jnp.inf)
            peak = jnp.maximum(jnp.max(scores, axis=1, keepdims=True), own)
            exps = jnp.exp(scores - peak)
            own_exp = jnp.exp(own - peak)
            total = jnp.sum(exps, axis=1, keepdims=True) + own_exp
            weights = (exps / total).astype(jnp.bfloat16)
            own_weight = (own_exp / total).astype(jnp.bfloat16).astype(jnp.float32)
            mixed = jnp.dot(weights, vc[r, g], preferred_element_type=jnp.float32)
            mixed = mixed + own_weight * v_new
            ag[pl.ds(pl.multiple_of(g * 256 + i * 32 + r * 16, 16), 16), :] = mixed.astype(jnp.bfloat16)
    for g in range(3):
        gathers.append(Gather(ag, g * 256, 32, z, x, a_send, a_recv, g))
        sends += gathers[g].start()
    for gather in gathers:
        sends += gather.forward()

    theirs = pl.multiple_of((1 - c) * 8, 8)
    ours = pl.multiple_of(c * 8, 8)

    def term_copy(t):
        return pltpu.make_async_remote_copy(
            terms.at[t, pl.ds(theirs, 8)], other_terms.at[t], t_send.at[t], t_recv.at[t],
            device_id={"gy": 1 - c}, device_id_type=MESH,
        )

    width = 16 * HD
    for g in range(3):
        gathers[g].wait()
        agf[...] = ag[g * 256 : (g + 1) * 256, :].astype(jnp.float32)
        for h in range(16):
            ab[:, h * HD : (h + 1) * HD] = agf[pl.ds(h, 16, stride=16), :].astype(jnp.bfloat16)

        @pl.loop(0, n_o)
        def _(t):
            if g == 0:
                wo_copy(t).wait()
            value = lax.dot_general(
                ab[...], wo[t, :, g * width : (g + 1) * width], NT, preferred_element_type=jnp.float32
            )
            terms[t] = value if g == 0 else terms[t] + value
            if g == 2:
                term_copy(t).start()

    for t in range(n_o):
        term_copy(t).wait_recv()
        out_ref[:, t * O_CHUNK : (t + 1) * O_CHUNK] = (
            terms[t, pl.ds(ours, 8), :] + other_terms[t]
        ).astype(jnp.bfloat16)

    for copy in sends:
        copy.wait_send()
    away.wait_send()
    for t in range(n_o):
        term_copy(t).wait_send()
    for o in range(4):
        itself = jnp.logical_and(c == half, mine == o)

        @pl.when(jnp.logical_not(itself))
        def _():
            message(o).wait_send()


def fused(tokens, query_weight, key_weight, value_weight, output_weight, key_cache, value_cache, lengths):
    depth = tokens.shape[1]
    n_q = query_weight.shape[0] // Q_CHUNK
    n_o = output_weight.shape[0] // O_CHUNK
    head_w = output_weight.shape[1]
    anywhere = pl.BlockSpec(memory_space=pl.ANY)
    in_vmem = pl.BlockSpec(memory_space=pltpu.VMEM)
    f32, bf16, dma = jnp.float32, jnp.bfloat16, pltpu.SemaphoreType.DMA
    return pl.pallas_call(
        kernel,
        out_shape=jax.ShapeDtypeStruct((GX, output_weight.shape[0]), bf16),
        in_specs=[pl.BlockSpec(memory_space=pltpu.SMEM), in_vmem] + [anywhere] * 6,
        out_specs=in_vmem,
        scratch_shapes=[
            pltpu.VMEM((n_q, Q_CHUNK, depth), bf16),
            pltpu.VMEM((256, depth), bf16),
            pltpu.VMEM((n_o, O_CHUNK, head_w), bf16),
            pltpu.VMEM(key_cache.shape, bf16),
            pltpu.VMEM(value_cache.shape, bf16),
            pltpu.VMEM((TOK_ROWS, HD), f32),
            pltpu.VMEM((GX * TOK_ROWS, HD), bf16),
            pltpu.VMEM((GX * TOK_ROWS, HD), f32),
            pltpu.VMEM((16, depth), bf16),
            pltpu.VMEM((256, 128), f32),
            pltpu.VMEM((128, 128), f32),
            pltpu.VMEM((128, 128), bf16),
            pltpu.VMEM((128, 128), bf16),
            pltpu.VMEM((96, 128), f32),
            pltpu.VMEM((GX * 96, 128), bf16),
            pltpu.VMEM((GX * 32, 128), f32),
            pltpu.VMEM((16, 16 * HD), bf16),
            pltpu.VMEM((n_o, 16, O_CHUNK), f32),
            pltpu.VMEM((n_o, 8, O_CHUNK), f32),
            dma((n_q,)), dma((2,)), dma((n_o,)), dma((2,)),
            dma((7,)), dma((GX,)), dma((1,)), dma((1,)), dma((4,)), dma((4,)),
            dma((21,)), dma((3 * GX,)), dma((n_o,)), dma((n_o,)),
        ],
        compiler_params=pltpu.CompilerParams(
            collective_id=0, has_side_effects=True, vmem_limit_bytes=60 * 2**20
        ),
        cost_estimate=pl.CostEstimate(
            flops=1 << 30, bytes_accessed=54 << 20, transcendentals=1 << 15
        ),
    )(lengths, tokens, query_weight, key_weight, value_weight, output_weight, key_cache, value_cache)


def fits_fused(tokens, query_weight, key_weight, output_weight, key_cache):
    return (
        lax.axis_size("gx") == GX
        and lax.axis_size("gy") == 2
        and tokens.shape == (2, TOK_ROWS * HD // 2)
        and query_weight.shape[0] == 12 * HD
        and key_weight.shape[0] == 96
        and key_cache.shape == (2, 3, 256, HD)
        and output_weight.shape == (2048, 48 * HD)
    )


def rotate(values, positions):
    half_width = values.shape[-1] // 2
    freqs = jnp.exp(
        -(jnp.arange(half_width, dtype=jnp.float32) * (2.0 / values.shape[-1])) * math.log(500000.0)
    )
    angles = positions[:, None] * freqs[None, :]
    cosine = jnp.cos(angles)[:, None, :]
    sine = jnp.sin(angles)[:, None, :]
    first = values[..., :half_width]
    second = values[..., half_width:]
    return jnp.concatenate(
        [first * cosine - second * sine, second * cosine + first * sine], axis=-1
    )


def product(row_piece, matrix):
    return lax.dot_general(
        row_piece, matrix, (((1,), (1,)), ((), ())), preferred_element_type=jnp.float32
    )


def local(
    tokens, query_weight, key_weight, value_weight, output_weight, key_cache, value_cache, lengths
):
    if fits_fused(tokens, query_weight, key_weight, output_weight, key_cache):
        return fused(
            tokens, query_weight, key_weight, value_weight, output_weight, key_cache, value_cache, lengths
        )
    rows_here = tokens.shape[0]
    width_gx = lax.axis_size("gx")
    width_query = query_weight.shape[0]
    width_key = key_weight.shape[0]
    width_all = width_query + 2 * width_key
    local_heads = key_cache.shape[1]
    group_size = HQ // KVH
    row_piece = lax.all_gather(tokens, "gx", axis=0, tiled=True)
    partial_value = jnp.concatenate(
        [
            product(row_piece, query_weight),
            product(row_piece, key_weight),
            product(row_piece, value_weight),
        ],
        axis=1,
    )
    summed = lax.psum(partial_value, "gy").astype(jnp.bfloat16)
    owned = lax.all_to_all(summed, "gx", split_axis=0, concat_axis=1, tiled=True)
    blocks = owned.reshape(rows_here, width_gx, width_all)
    query_all = blocks[:, :, :width_query].reshape(rows_here, HQ, HD)
    key_all = blocks[:, :, width_query : width_query + width_key].reshape(rows_here, KVH, HD)
    value_all = blocks[:, :, width_query + width_key :].reshape(rows_here, KVH, HD)
    shard = lax.axis_index("gy")
    query_part = lax.dynamic_slice_in_dim(
        query_all, shard * local_heads * group_size, local_heads * group_size, 1
    )
    key_part = lax.dynamic_slice_in_dim(key_all, shard * local_heads, local_heads, 1)
    value_part = lax.dynamic_slice_in_dim(value_all, shard * local_heads, local_heads, 1)
    positions = lengths.astype(jnp.float32)
    query_rot = rotate(query_part.astype(jnp.float32), positions).astype(jnp.bfloat16)
    query_rot = query_rot.reshape(rows_here, local_heads, group_size, HD)
    key_rot = rotate(key_part.astype(jnp.float32), positions).astype(jnp.bfloat16)
    scale = HD ** (-0.5)
    own_score = (
        jnp.einsum("rgqd,rgd->rgq", query_rot, key_rot, preferred_element_type=jnp.float32) * scale
    )
    cache_len = key_cache.shape[2]
    scores = (
        jnp.einsum("rgqd,rgpd->rgqp", query_rot, key_cache, preferred_element_type=jnp.float32)
        * scale
    )
    valid_keys = jnp.arange(cache_len)[None, None, None, :] < lengths[:, None, None, None]
    scores = jnp.where(valid_keys, scores, -jnp.inf)
    peak = jnp.maximum(jnp.max(scores, axis=-1), own_score)
    exps = jnp.exp(scores - peak[..., None])
    own_exp = jnp.exp(own_score - peak)
    total = jnp.sum(exps, axis=-1) + own_exp
    weights = (exps / total[..., None]).astype(jnp.bfloat16)
    mixed = jnp.einsum("rgqp,rgpd->rgqd", weights, value_cache, preferred_element_type=jnp.float32)
    own_weight = (own_exp / total).astype(jnp.bfloat16)
    mixed = (
        mixed
        + own_weight.astype(jnp.float32)[..., None] * value_part.astype(jnp.float32)[:, :, None, :]
    )
    attended = mixed.astype(jnp.bfloat16).reshape(rows_here, local_heads * group_size * HD)
    terms = product(lax.all_gather(attended, "gx", axis=0, tiled=True), output_weight)
    return lax.psum_scatter(terms, "gy", scatter_dimension=0, tiled=True).astype(jnp.bfloat16)


def solution(mesh):
    in_specs = (
        P(("groups", "gx"), "gy"),
        P("gx", "gy"),
        P("gx", "gy"),
        P("gx", "gy"),
        P("gx", "gy"),
        P(("groups", "gx"), "gy", None, None),
        P(("groups", "gx"), "gy", None, None),
        P(("groups", "gx")),
    )
    out_specs = P(("groups", "gy"), "gx")
    return jax.shard_map(local, mesh=mesh, in_specs=in_specs, out_specs=out_specs, check_vma=False)
```
